32 devices in a mesh: seq: 16 (over z, y, core), tensor: 2 (over x).
Axes of the slice: x: 2, y: 2, z: 4, core: 2. Of those that a mesh axis runs over, the one named last changes fastest.
Arguments:
- trunk: bfloat16 [2, 1024, 1536], P(None, 'seq', 'tensor'), may hold values from -12 to 12
- w_out: bfloat16 [1536, 1536], P('tensor', 'seq'), may hold values from -1 to 1
- gain_coarse: float32 [1536], replicated, may hold values from 0.1 to 1.9
- w_conv1: bfloat16 [5, 1536, 1536], P(None, 'seq', 'tensor'), may hold values from -0.0625 to 0.0625
- w_up: bfloat16 [1536, 2, 768], P('seq', None, 'tensor'), may hold values from -0.15625 to 0.15625
- skip: bfloat16 [2, 2048, 768], P(None, 'seq', 'tensor'), may hold values from -12 to 12
- gain_fine: float32 [768], replicated, may hold values from 0.1 to 1.9
- w_conv2: bfloat16 [5, 768, 768], P(None, 'seq', 'tensor'), may hold values from -0.09375 to 0.09375
- cotangent: bfloat16 [2, 2048, 768], P(None, 'seq', 'tensor'), may hold values from -6 to 6
Outputs:
- decoded: bfloat16 [2, 2048, 768], P(None, 'seq', 'tensor')
- skip_grad: bfloat16 [2, 2048, 768], P(None, 'seq', 'tensor')
- trunk_grad: bfloat16 [2, 1024, 1536], P(None, 'seq', 'tensor')
The draws below stay inside these ranges and needn't reach their ends.
All inputs are finite; a program needn't handle non-finite values.
Results may differ from the reference program's by a relative error of at most 0.02.
Values may be sent and summed in bfloat16 or wider, within the bound.
A program may use at most 64 MiB of HBM per device.

```python
import math
import jax
import jax.numpy as jnp
from jax import lax

D_TRUNK = 1536
C_COARSE = 1536
C_FINE = 768
SEQS = 2
LENGTH = 1024
N_TENSOR = 2


def log_scales(key, shape):
    return jnp.exp(jax.random.uniform(key, shape, jnp.float32, math.log(0.3), math.log(3.0)))


def draw_trunk(key, part):
    key_a, key_b = jax.random.split(key, 2)
    shape = (SEQS, LENGTH, D_TRUNK)
    rows = log_scales(key_b, (SEQS, LENGTH, 1))
    values = jax.random.normal(key_a, shape, jnp.float32) * rows
    return jnp.clip(values, -12.0, 12.0).astype(jnp.bfloat16)


def draw_w_out(key, part):
    key_a, key_b = jax.random.split(key)
    shape = (D_TRUNK, C_COARSE)
    cols = log_scales(key_b, (1, C_COARSE)) * D_TRUNK ** (-0.5)
    values = jax.random.normal(key_a, shape, jnp.float32) * cols
    return jnp.clip(values, -1.0, 1.0).astype(jnp.bfloat16)


def draw_skip(key, part):
    key_a, key_b = jax.random.split(key, 2)
    shape = (SEQS, 2 * LENGTH, C_FINE)
    cols = log_scales(key_b, (1, 1, C_FINE))
    values = jax.random.normal(key_a, shape, jnp.float32) * cols
    return jnp.clip(values, -12.0, 12.0).astype(jnp.bfloat16)


def block_levels(rng, extent, pieces, least, high):
    loudness, own = 1.0, jax.random.fold_in(rng, 6)
    for position, blocks in pieces:
        heights = jnp.exp(jax.random.uniform(jax.random.fold_in(own, position), (blocks,), jnp.float32, least / len(pieces), high / len(pieces)))
        loudness = loudness * jnp.repeat(heights, extent[position] // blocks).reshape([-1 if axis == position else 1 for axis in range(len(extent))])
    return loudness


def gaussian(rng, extent, spread, bound, cuts=(), held_as=jnp.bfloat16):
    drawn = jax.random.normal(rng, extent, jnp.float32) * spread
    if len(cuts) > 0:
        drawn = block_levels(rng, extent, cuts, -0.22, 0.18) * drawn
    return jnp.clip(drawn, min=-bound, max=bound).astype(held_as)


def setup_inputs(seed: int = 0) -> dict:
    seeds = jax.random.split(jax.random.key(seed), 10)
    trunk = draw_trunk(jax.random.fold_in(seeds[9], 71), 0)
    w_out = draw_w_out(jax.random.fold_in(seeds[9], 71), 0)
    gain_coarse = jnp.clip(1.0 + 0.18 * jax.random.normal(seeds[2], (C_COARSE,), jnp.float32), 0.1, 1.9)
    w_conv1 = gaussian(seeds[3], (5, C_COARSE, C_COARSE), (5 * C_COARSE) ** -0.5, 0.0625, ((1, 16), (2, 2)))
    w_up = gaussian(seeds[4], (C_COARSE, 2, C_FINE), C_COARSE ** -0.5, 0.15625, ((0, 16), (2, 2)))
    skip = draw_skip(jax.random.fold_in(seeds[9], 71), 0)
    gain_fine = jnp.clip(1.0 + 0.18 * jax.random.normal(seeds[6], (C_FINE,), jnp.float32), 0.1, 1.9)
    w_conv2 = gaussian(seeds[7], (5, C_FINE, C_FINE), (5 * C_FINE) ** -0.5, 0.09375, ((1, 16), (2, 2)))
    cotangent = gaussian(seeds[8], (SEQS, 2 * LENGTH, C_FINE), 1.0, 6.0, ((1, 16), (2, 2)))
    return {"trunk": trunk, "w_out": w_out, "gain_coarse": gain_coarse, "w_conv1": w_conv1, "w_up": w_up, "skip": skip, "gain_fine": gain_fine, "w_conv2": w_conv2, "cotangent": cotangent}


EPS = 1e-06

def matmul(left, right):
    flat = jnp.dot(left.reshape(-1, left.shape[-1]), right, preferred_element_type=jnp.float32)
    return flat.reshape(left.shape[:-1] + (right.shape[-1],))

def rounded(value):
    return lax.optimization_barrier(value.astype(jnp.bfloat16)).astype(jnp.float32)

def activate(field, gain):
    scaled = field * lax.rsqrt(lax.optimization_barrier(jnp.mean(field * field, axis=-1, keepdims=True)) + EPS)
    return jax.nn.gelu(scaled * gain)

def conv_ahead(act, weight):
    length = act.shape[1]
    padded = jnp.pad(act, ((0, 0), (2, 2), (0, 0)))
    total = jnp.zeros(act.shape[:2] + (weight.shape[2],), jnp.float32)
    for k in range(5):
        total = total + matmul(padded[:, k:k + length], weight[k])
    return total

def conv_behind(grad, weight):
    length = grad.shape[1]
    padded = jnp.pad(grad, ((0, 0), (2, 2), (0, 0)))
    total = jnp.zeros(grad.shape[:2] + (weight.shape[1],), jnp.float32)
    for k in range(5):
        total = total + matmul(padded[:, 4 - k:4 - k + length], weight[k].T)
    return total

def norm_vjp(field, gain, grad):

    def apply(value):
        return activate(value, gain)
    _, pull = jax.vjp(apply, field.astype(jnp.float32))
    return pull(grad)[0]

def reference(trunk, w_out, gain_coarse, w_conv1, w_up, skip, gain_fine, w_conv2, cotangent):
    groups = N_TENSOR
    hpart = D_TRUNK // groups
    cpart = C_COARSE // groups
    fpart = C_FINE // groups
    seqs = trunk.shape[0]
    length = trunk.shape[1]
    projected = jnp.zeros((seqs, length, C_COARSE), jnp.float32)
    for g in range(groups):
        projected = projected + rounded(matmul(trunk[:, :, g * hpart:(g + 1) * hpart], w_out[g * hpart:(g + 1) * hpart]))
    projected = projected.astype(jnp.bfloat16)
    act_coarse = activate(projected.astype(jnp.float32), gain_coarse).astype(jnp.bfloat16)
    lifted = (projected.astype(jnp.float32) + conv_ahead(act_coarse, w_conv1)).astype(jnp.bfloat16)
    upper = matmul(lifted, w_up.reshape(C_COARSE, 2 * C_FINE)).reshape(seqs, 2 * length, C_FINE)
    merged = (upper + skip.astype(jnp.float32)).astype(jnp.bfloat16)
    act_fine = activate(merged.astype(jnp.float32), gain_fine).astype(jnp.bfloat16)
    decoded = (merged.astype(jnp.float32) + conv_ahead(act_fine, w_conv2)).astype(jnp.bfloat16)
    back_fine = jnp.zeros((seqs, 2 * length, C_FINE), jnp.float32)
    for g in range(groups):
        back_fine = back_fine + rounded(conv_behind(cotangent[:, :, g * fpart:(g + 1) * fpart], w_conv2[:, :, g * fpart:(g + 1) * fpart]))
    skip_grad = (cotangent.astype(jnp.float32) + norm_vjp(merged, gain_fine, back_fine)).astype(jnp.bfloat16)
    lifted_grad = jnp.zeros((seqs, length, C_COARSE), jnp.float32)
    for g in range(groups):
        piece = skip_grad[:, :, g * fpart:(g + 1) * fpart].reshape(seqs, length, 2 * fpart)
        wpiece = w_up[:, :, g * fpart:(g + 1) * fpart].reshape(C_COARSE, 2 * fpart)
        lifted_grad = lifted_grad + rounded(matmul(piece, wpiece.T))
    lifted_grad = lifted_grad.astype(jnp.bfloat16)
    back_coarse = jnp.zeros((seqs, length, C_COARSE), jnp.float32)
    for g in range(groups):
        back_coarse = back_coarse + rounded(conv_behind(lifted_grad[:, :, g * cpart:(g + 1) * cpart], w_conv1[:, :, g * cpart:(g + 1) * cpart]))
    projected_grad = (lifted_grad.astype(jnp.float32) + norm_vjp(projected, gain_coarse, back_coarse)).astype(jnp.bfloat16)
    trunk_grad = matmul(projected_grad, w_out.T).astype(jnp.bfloat16)
    return (decoded, skip_grad, trunk_grad)
```

```python
import functools

import jax
import jax.numpy as jnp
from jax import lax
from jax.experimental import pallas as pl
from jax.experimental.pallas import tpu as pltpu
from jax.sharding import PartitionSpec as P

C_COARSE = 1536
C_FINE = 768


EPS = 1e-06


def extended(shard, sides, width):
    for axis, dim in sides:
        size, length = (lax.axis_size(axis), shard.shape[dim])
        up = [(i, (i + 1) % size) for i in range(size - 1)]
        down = [(j, i) for i, j in up]
        last = lax.slice_in_dim(shard, length - width, length, axis=dim)
        leading = lax.slice_in_dim(shard, 0, width, axis=dim)
        before = lax.ppermute(last, axis, up)
        after = lax.ppermute(leading, axis, down)
        shard = jnp.concatenate([before, shard, after], axis=dim)
    return shard


def matmul(left, right):
    return lax.dot_general(
        left, right, (((left.ndim - 1,), (0,)), ((), ())), preferred_element_type=jnp.float32
    )


def matmul_back(left, right):
    return lax.dot_general(
        left,
        right,
        (((left.ndim - 1,), (right.ndim - 1,)), ((), ())),
        preferred_element_type=jnp.float32,
    )


def activate(field, gain):
    scaled = field * lax.rsqrt(jnp.mean(field * field, axis=-1, keepdims=True) + EPS)
    return jax.nn.gelu(scaled * gain)


def widen(field):
    return extended(field, (("seq", 1),), 2)


def spread(field):
    return lax.all_gather(field, "tensor", axis=2, tiled=True)


def conv_rows(total, wide, piece):
    length = wide.shape[1] - 4
    for k in range(5):
        total = total + matmul(wide[:, k : k + length], piece[k])
    return total


def conv_back(wide_grad, piece):
    length = wide_grad.shape[1] - 4
    total = jnp.zeros((wide_grad.shape[0], length, piece.shape[1]), jnp.float32)
    for k in range(5):
        total = total + matmul_back(wide_grad[:, 4 - k : 4 - k + length], piece[k])
    return total


def norm_back(partial_grad, field_full, gain, rank, part):
    field = field_full.astype(jnp.float32)
    start = rank * part
    whole = lax.psum(partial_grad.astype(jnp.bfloat16), "tensor").astype(jnp.float32)

    def apply(value):
        return activate(value, gain)

    _, pull = jax.vjp(apply, field)
    return lax.dynamic_slice_in_dim(pull(whole)[0], start, part, 2)


def per_device(trunk, w_out, gain_coarse, w_conv1, w_up, skip, gain_fine, w_conv2, cotangent):
    rank = lax.axis_index("tensor")
    part_coarse = C_COARSE // lax.axis_size("tensor")
    part_fine = C_FINE // lax.axis_size("tensor")
    seqs = trunk.shape[0]
    slab = trunk.shape[1]
    out_w, up_w, conv2_w = (
        lax.all_gather(w_out, "seq", axis=1, tiled=True),
        lax.all_gather(w_up, "seq", axis=0, tiled=True),
        lax.all_gather(w_conv2, "seq", axis=1, tiled=True),
    )
    partial_proj = matmul(trunk, out_w)
    projected = lax.psum_scatter(
        partial_proj.astype(jnp.bfloat16), "tensor", scatter_dimension=2, tiled=True
    )
    projected_full = lax.all_gather(projected, "tensor", axis=2, tiled=True)
    act_coarse = activate(projected_full.astype(jnp.float32), gain_coarse).astype(jnp.bfloat16)
    coarse_wide = widen(act_coarse)
    empty_coarse = jnp.zeros((seqs, slab, part_coarse), jnp.float32)
    mixed_coarse = conv_rows(
        empty_coarse, coarse_wide, lax.all_gather(w_conv1, "seq", axis=1, tiled=True)
    )
    lifted = (projected.astype(jnp.float32) + mixed_coarse).astype(jnp.bfloat16)
    lifted_full = spread(lifted)
    upper = matmul(lifted_full, up_w).reshape(seqs, 2 * slab, part_fine)
    merged = (upper + skip.astype(jnp.float32)).astype(jnp.bfloat16)
    merged_full = spread(merged)
    act_fine = activate(merged_full.astype(jnp.float32), gain_fine).astype(jnp.bfloat16)
    fine_wide = widen(act_fine)
    empty_fine = jnp.zeros((seqs, 2 * slab, part_fine), jnp.float32)
    mixed_fine = conv_rows(empty_fine, fine_wide, conv2_w)
    decoded = (merged.astype(jnp.float32) + mixed_fine).astype(jnp.bfloat16)
    cot_wide = widen(cotangent)
    back_fine = conv_back(cot_wide, conv2_w)
    skip_grad = (
        cotangent.astype(jnp.float32)
        + norm_back(back_fine, merged_full, gain_fine, rank, part_fine)
    ).astype(jnp.bfloat16)
    folded = skip_grad.reshape(seqs, slab, 2 * part_fine)
    up_partial = matmul_back(folded, up_w.reshape(up_w.shape[0], 2 * part_fine))
    lifted_grad = lax.psum_scatter(
        up_partial.astype(jnp.bfloat16), "tensor", scatter_dimension=2, tiled=True
    )
    grad_wide = widen(lifted_grad)
    back_coarse = conv_back(grad_wide, lax.all_gather(w_conv1, "seq", axis=1, tiled=True))
    projected_grad = (
        lifted_grad.astype(jnp.float32)
        + norm_back(back_coarse, projected_full, gain_coarse, rank, part_coarse)
    ).astype(jnp.bfloat16)
    grad_full = spread(projected_grad)
    trunk_grad = matmul_back(grad_full, out_w).astype(jnp.bfloat16)
    return (decoded, skip_grad, trunk_grad)


PIECES = 8
LINE = 4
HALO = 8


def fits(mesh):
    return mesh.shape["seq"] == 4 * LINE and mesh.shape["tensor"] == 2


def gelu_parts(u):
    c = 0.7978845608028654
    th = jnp.tanh(c * (u + 0.044715 * (u * u * u)))
    return 0.5 * (1.0 + th), th, c


def gelu(u):
    half, _, _ = gelu_parts(u)
    return u * half


def gelu_slope(u):
    half, th, c = gelu_parts(u)
    return half + 0.5 * u * (1.0 - th * th) * c * (1.0 + 3.0 * 0.044715 * (u * u))


def dot(a, b):
    return jnp.dot(a, b, preferred_element_type=jnp.float32)


def dot_t(a, b):
    return lax.dot_general(a, b, (((1,), (1,)), ((), ())), preferred_element_type=jnp.float32)


def fused_kernel(
    trunk, w_own, w2_own, skip, cot, gain_c, gain_f,
    decoded, skip_grad, trunk_grad,
    wb, w2, center, halo, ext, skipf, cotf, pp, pp_in, proj, act, accf, lifted, merged, actf,
    bf, bf_in, accd, sgf, sgb, ug, ug_in, lgf, lgc, lgk, bc, bc_in, pg,
    rsem, ssem, lsem, hs, hr, xs, xr,
):
    s = lax.axis_index("seq")
    x = lax.axis_index("tensor")
    z = s // 4
    y = (s // 2) % 2
    c = s % 2
    rows = ext.shape[0]
    per = rows // 2
    slab = per - 2 * HALO
    half = wb.shape[2]
    quarter = half // 2
    seqs = 2
    MESH = pl.DeviceIdType.MESH
    bf16 = jnp.bfloat16
    n_seq = 4 * LINE

    def near(dev):
        return {"seq": dev}

    ydev = s + 2 - 4 * y
    cdev = s + 1 - 2 * c
    xdev = {"tensor": 1 - x}

    own_w = pltpu.make_async_copy(
        w_own, wb.at[:, pl.ds(pl.multiple_of(s * 96, 96), 96), :], lsem.at[0]
    )
    own_w2 = pltpu.make_async_copy(
        w2_own, w2.at[:, pl.ds(pl.multiple_of(s * 48, 48), 48), :], lsem.at[1]
    )
    mine = [pltpu.make_async_copy(r, center.at[i], lsem.at[2 + i]) for i, r in enumerate((trunk, skip, cot))]
    for copy in [own_w2, own_w] + mine:
        copy.start()

    barrier = pltpu.get_barrier_semaphore()
    for dev in (near(ydev), near(cdev), xdev):
        pl.semaphore_signal(barrier, inc=1, device_id=dev, device_id_type=MESH)
    for ok, dev in ((z > 0, s - 4), (z < LINE - 1, s + 4), (s > 0, s - 1), (s < n_seq - 1, s + 1)):

        @pl.when(ok)
        def _(dev=dev):
            pl.semaphore_signal(barrier, inc=1, device_id=near(dev), device_id_type=MESH)

    one = jnp.int32(1)
    zero = jnp.int32(0)
    count = (
        3
        + jnp.where(z > 0, one, zero)
        + jnp.where(z < LINE - 1, one, zero)
        + jnp.where(s > 0, one, zero)
        + jnp.where(s < n_seq - 1, one, zero)
    )
    pl.semaphore_wait(barrier, count)

    def halo_copy(i, side, dev):
        lo = slab - 16 if side == 0 else 0
        return pltpu.make_async_remote_copy(
            src_ref=center.at[i, :, pl.ds(lo, 16), :],
            dst_ref=halo.at[i, side],
            send_sem=hs.at[i, side],
            recv_sem=hr.at[i, side],
            device_id=near(dev),
            device_id_type=MESH,
        )

    def ref(p, owner, wide):
        if wide:
            return w2.at[:, pl.ds(pl.multiple_of(owner * 48, 48), 48), :]
        return wb.at[p - 1, pl.ds(pl.multiple_of(owner * 96, 96), 96), :]

    def send(p, owner, wide, way, dev):
        return pltpu.make_async_remote_copy(
            src_ref=ref(p, owner, wide),
            dst_ref=ref(p, owner, wide),
            send_sem=ssem.at[p, owner, way],
            recv_sem=rsem.at[p, owner],
            device_id=near(dev),
            device_id_type=MESH,
        )

    def routes():
        out = []
        for d in range(LINE):
            for sign in (1, -1) if d else (0,):
                out.append((d, sign, False))
                out.append((d, sign, True))
        return out

    def each(p, d, sign, across, act_on):
        zz = z - sign * d
        base = s - 4 * sign * d
        owner = base + 2 - 4 * y if across else base
        there = (zz >= 0) & (zz < LINE) & (p >= 0) & (p < PIECES)
        for wide in (True, False):

            @pl.when(there & ((p == 0) if wide else (p > 0)))
            def _(wide=wide):
                act_on(p, owner, wide, d, sign, across)

    def targets(p, owner, wide, sign, across, do):
        if not across:
            if sign >= 0:

                @pl.when(z < LINE - 1)
                def _():
                    do(send(p, owner, wide, 0, s + 4))

            if sign <= 0:

                @pl.when(z > 0)
                def _():
                    do(send(p, owner, wide, 1, s - 4))

            do(send(p, owner, wide, 2, ydev))
        do(send(p, owner, wide, 3, cdev))

    def forward(p, owner, wide, d, sign, across):
        if d or across:
            send(p, owner, wide, 3, cdev).wait_recv()
        targets(p, owner, wide, sign, across, lambda copy: copy.start())

    def drain(p, owner, wide, d, sign, across):
        targets(p, owner, wide, sign, across, lambda copy: copy.wait_send())

    def step(t):
        for d, sign, across in routes():
            each(t - d - (1 if across else 0), d, sign, across, forward)

    def from_core(p, wide):
        def body(i, carry):
            owner = 2 * i + 1 - c
            send(p, owner, wide, 3, cdev).wait_recv()
            return carry

        lax.fori_loop(0, 2 * LINE, body, 0)

    def exchange(i, src, dst):
        return pltpu.make_async_remote_copy(
            src_ref=src,
            dst_ref=dst,
            send_sem=xs.at[i],
            recv_sem=xr.at[i],
            device_id=xdev,
            device_id_type=MESH,
        )

    def loop(n, body):
        def run(i, carry):
            body(i)
            return carry

        lax.fori_loop(0, n, run, 0)

    own_w2.wait()
    own_w.wait()
    for copy in mine:
        copy.wait()
    for i in range(3):
        for side, ok, dev in ((0, s < n_seq - 1, s + 1), (1, s > 0, s - 1)):

            @pl.when(ok)
            def _(i=i, side=side, dev=dev):
                halo_copy(i, side, dev).start()

    loop(4, step)

    for i in range(3):
        for side, ok in ((0, s > 0), (1, s < n_seq - 1)):

            @pl.when(ok)
            def _(i=i, side=side):
                halo_copy(i, side, cdev).wait_recv()

            @pl.when(jnp.logical_not(ok))
            def _(i=i, side=side):
                halo[i, side] = jnp.zeros(halo.shape[2:], bf16)

    for i in range(3):
        for q in range(seqs):
            before = halo[i, 0, q].astype(jnp.float32)[16 - HALO :]
            after = halo[i, 1, q].astype(jnp.float32)[:HALO]
            whole = jnp.concatenate([before, center[i, q].astype(jnp.float32), after], axis=0)
            if i == 0:
                ext[pl.ds(q * per, per), :] = whole.astype(bf16)
            elif i == 1:
                skipf[pl.ds(q * per, per), :] = whole
            else:
                cotf[pl.ds(q * per, per), :] = whole

    def inside(start, size):
        r = start + lax.broadcasted_iota(jnp.int32, (size, 1), 0)
        at = jnp.where(r >= per, r - per, r) + s * slab - HALO
        return (at >= 0) & (at < n_seq * slab)

    lax.fori_loop(4, 6, lambda t, k: (step(t), k)[1], 0)
    from_core(0, True)
    from_core(1, False)

    def project(n):
        cols = pl.ds(pl.multiple_of(n * 256, 256), 256)
        pp[:, cols] = dot_t(ext[...], wb[0, cols, :]).astype(bf16)

    loop(2 * half // 256, project)
    send_pp = exchange(0, pp, pp_in)
    send_pp.start()

    step(6)

    def roll(v, shift):
        return pltpu.roll(v, shift % rows, 0)

    c0 = cotf[:, :quarter]
    c1 = cotf[:, quarter:]
    b0, b1 = c0.astype(bf16), c1.astype(bf16)
    up0, up1 = roll(c0, -1).astype(bf16), roll(c1, -1).astype(bf16)
    dn0, dn1 = roll(c0, 1).astype(bf16), roll(c1, 1).astype(bf16)
    even = (up0, b1, b0, dn1, dn0)
    odd = (up1, up0, b1, b0, dn1)

    def back_fine(n):
        cols = pl.ds(pl.multiple_of(n * 256, 256), 256)
        for par, taps in ((0, even), (1, odd)):
            total = dot_t(taps[0], w2[0, cols, :])
            for k in range(1, 5):
                total = total + dot_t(taps[k], w2[k, cols, :])
            bf[par, :, cols] = total.astype(bf16)

    loop(half // 256, back_fine)
    send_bf = exchange(1, bf, bf_in)
    send_bf.start()

    send_pp.wait_recv()

    def norm(f):
        return lax.rsqrt(jnp.mean(f * f, axis=-1, keepdims=True) + EPS)

    def coarse(i):
        at = pl.ds(pl.multiple_of(i * 32, 32), 32)
        f = (pp[at, :].astype(jnp.float32) + pp_in[at, :].astype(jnp.float32)).astype(bf16).astype(jnp.float32)
        proj[at, :] = f
        a = gelu(f * norm(f) * gain_c[...])
        act[at, :] = jnp.where(inside(i * 32, 32), a, 0.0).astype(bf16)

    loop(rows // 32, coarse)
    xhalf = pl.ds(pl.multiple_of(x * half, half), half)
    accf[...] = proj[:, xhalf]

    def tap_ahead(k):
        step(7 + k)
        from_core(3 + k, False)
        for n in range(half // 256):
            cols = pl.ds(n * 256, 256)
            accf[:, cols] += pltpu.roll(dot(act[...], wb[2 + k, :, cols]), lax.rem(rows + 2 - k, rows), 0)

    loop(5, tap_ahead)
    lifted[:, xhalf] = accf[...].astype(bf16)
    send_lifted = exchange(2, lifted.at[:, xhalf], lifted.at[:, xhalf])
    send_lifted.start()
    from_core(2, False)
    exchange(2, lifted.at[:, pl.ds(pl.multiple_of((1 - x) * half, half), half)], lifted.at[:, pl.ds(pl.multiple_of((1 - x) * half, half), half)]).wait_recv()
    xq = pl.ds(pl.multiple_of(x * quarter, quarter), quarter)
    oq = pl.ds(pl.multiple_of((1 - x) * quarter, quarter), quarter)
    for n in range(half // 384):
        cols = pl.ds(n * 384, 384)
        m = (dot(lifted[...], wb[1, :, cols]) + skipf[:, cols]).astype(bf16)
        merged[n, :, xq] = m
        accd[:, cols] = m.astype(jnp.float32)
    send_merged = exchange(3, merged.at[:, :, xq], merged.at[:, :, xq])
    send_merged.start()
    send_bf.wait_recv()
    exchange(3, merged.at[:, :, oq], merged.at[:, :, oq]).wait_recv()

    def pull(f, gain, grad):
        r = norm(f)
        dn = grad * gelu_slope(f * r * gain) * gain
        return r * dn - f * (r * r * r * jnp.mean(dn * f, axis=-1, keepdims=True))

    def fine(i):
        at = pl.ds(pl.multiple_of(i * 32, 32), 32)
        for par in range(2):
            f = merged[par, at, :].astype(jnp.float32)
            u = f * norm(f) * gain_f[...]
            actf[par, at, :] = jnp.where(inside(i * 32, 32), gelu(u), 0.0).astype(bf16)
            g = bf[par, at, :].astype(jnp.float32) + bf_in[par, at, :].astype(jnp.float32)
            df = pull(f, gain_f[...], g)
            mine = jnp.where(x == 0, df[:, :quarter], df[:, quarter:])
            cols = pl.ds(par * quarter, quarter)
            v = cotf[at, cols] + mine
            sgf[at, cols] = v
            sgb[at, cols] = v.astype(bf16)

    loop(rows // 32, fine)

    def up_back(which, out):
        def body(n):
            cols = pl.ds(pl.multiple_of(n * 256, 256), 256)
            wrow = pl.ds(pl.multiple_of(which * half + n * 256, 256), 256)
            out[:, cols] = dot_t(sgb[...], wb[1, wrow, :]).astype(bf16)

        loop(half // 256, body)

    up_back(1 - x, ug)
    send_ug = exchange(4, ug, ug_in)
    send_ug.start()
    send_lifted.wait_send()
    up_back(x, lifted.at[:, pl.ds(0, half)])
    for q in range(seqs):
        skip_grad[q] = sgf[pl.ds(q * per + HALO, slab), :].astype(bf16)
    send_ug.wait_recv()

    def meet(i):
        at = pl.ds(pl.multiple_of(i * 32, 32), 32)
        v = lifted[at, :half].astype(jnp.float32) + ug_in[at, :].astype(jnp.float32)
        lgf[at, :] = jnp.where(inside(i * 32, 32), v, 0.0).astype(bf16).astype(jnp.float32)

    loop(rows // 32, meet)
    for q in range(seqs):
        lgc[pl.ds(q * slab, slab), xhalf] = lgf[pl.ds(q * per + HALO, slab), :].astype(bf16)
    send_lg = exchange(5, lgc.at[:, xhalf], lgc.at[:, xhalf])
    send_lg.start()

    def shifted(k):
        v = pltpu.roll(lgf[...], lax.rem(rows + k - 2, rows), 0)
        for q in range(seqs):
            lgk[k, pl.ds(q * slab, slab), :] = v[q * per + HALO : q * per + HALO + slab].astype(bf16)

    loop(5, shifted)

    def back_coarse(n):
        cols = pl.ds(pl.multiple_of(n * 256, 256), 256)
        total = dot_t(lgk[0], wb[2, cols, :])
        for k in range(1, 5):
            total = total + dot_t(lgk[k], wb[2 + k, cols, :])
        bc[:, cols] = total.astype(bf16)

    loop(2 * half // 256, back_coarse)
    send_bc = exchange(6, bc, bc_in)
    send_bc.start()

    e = {}
    for k in range(5):
        e[k] = [dot(actf[par], w2[k]) for par in range(2)]
        for par in range(2):
            fine_at = par - (k - 2)
            q = fine_at % 2
            shift = (fine_at - q) // 2
            v = e[k][par] if shift == 0 else roll(e[k][par], shift)
            accd[:, q * quarter : (q + 1) * quarter] += v
    for q in range(seqs):
        decoded[q] = accd[pl.ds(q * per + HALO, slab), :].astype(bf16)

    oth = pl.ds(pl.multiple_of((1 - x) * half, half), half)
    exchange(5, lgc.at[:, oth], lgc.at[:, oth]).wait_recv()
    send_bc.wait_recv()
    for q in range(seqs):

        def last(i, q=q):
            at = pl.ds(pl.multiple_of(q * slab + i * 32, 32), 32)
            f = proj[pl.ds(pl.multiple_of(q * per + HALO + i * 32, 8), 32), :]
            g = bc[at, :].astype(jnp.float32) + bc_in[at, :].astype(jnp.float32)
            pg[at, :] = (lgc[at, :].astype(jnp.float32) + pull(f, gain_c[...], g)).astype(bf16)

        loop(slab // 32, last)
    for n in range(half // 256):
        cols = pl.ds(n * 256, 256)
        v = dot(pg[...], wb[0, :, cols]).astype(bf16)
        for q in range(seqs):
            trunk_grad[q, :, cols] = v[q * slab : (q + 1) * slab]

    for copy in (send_pp, send_bf, send_merged, send_ug, send_lg, send_bc):
        copy.wait_send()
    for i in range(3):
        for side, ok, dev in ((0, s < n_seq - 1, s + 1), (1, s > 0, s - 1)):

            @pl.when(ok)
            def _(i=i, side=side, dev=dev):
                halo_copy(i, side, dev).wait_send()

    def finish(p):
        for d, sign, across in routes():
            each(p, d, sign, across, drain)

    loop(PIECES, finish)


def per_device_fused(trunk, w_out, gain_coarse, w_conv1, w_up, skip, gain_fine, w_conv2, cotangent):
    seqs, slab, half = trunk.shape
    quarter = half // 2
    n = lax.axis_size("seq")
    rows = seqs * (slab + 2 * HALO)
    w_own = jnp.concatenate([w_out.T[None], w_up.reshape(1, -1, half), w_conv1], axis=0)
    bf16, f32 = jnp.bfloat16, jnp.float32
    V = pltpu.VMEM
    out = jax.ShapeDtypeStruct((seqs, slab, half), bf16)
    vm = pl.BlockSpec(memory_space=pltpu.VMEM)
    anyw = pl.BlockSpec(memory_space=pl.ANY)
    decoded, skip_grad, trunk_grad = pl.pallas_call(
        fused_kernel,
        out_shape=(out, out, out),
        in_specs=[anyw] * 5 + [vm] * 2,
        out_specs=(vm, vm, vm),
        scratch_shapes=[
            V((7, 2 * half, half), bf16),
            V((5, half, quarter), bf16),
            V((3, seqs, slab, half), bf16),
            V((3, 2, seqs, 16, half), bf16),
            V((rows, half), bf16),
            V((rows, half), f32),
            V((rows, half), f32),
            V((rows, 2 * half), bf16),
            V((rows, 2 * half), bf16),
            V((rows, 2 * half), f32),
            V((rows, 2 * half), bf16),
            V((rows, half), f32),
            V((rows, 2 * half), bf16),
            V((2, rows, half), bf16),
            V((2, rows, half), bf16),
            V((2, rows, half), bf16),
            V((2, rows, half), bf16),
            V((rows, half), f32),
            V((rows, half), f32),
            V((rows, half), bf16),
            V((rows, half), bf16),
            V((rows, half), bf16),
            V((rows, half), f32),
            V((seqs * slab, 2 * half), bf16),
            V((5, seqs * slab, half), bf16),
            V((seqs * slab, 2 * half), bf16),
            V((seqs * slab, 2 * half), bf16),
            V((seqs * slab, 2 * half), bf16),
            pltpu.SemaphoreType.DMA((PIECES, n)),
            pltpu.SemaphoreType.DMA((PIECES, n, 4)),
            pltpu.SemaphoreType.DMA((5,)),
            pltpu.SemaphoreType.DMA((3, 2)),
            pltpu.SemaphoreType.DMA((3, 2)),
            pltpu.SemaphoreType.DMA((7,)),
            pltpu.SemaphoreType.DMA((7,)),
        ],
        compiler_params=pltpu.CompilerParams(
            collective_id=0, has_side_effects=True, vmem_limit_bytes=56 * 1024 * 1024
        ),
    )(
        trunk,
        w_own,
        w_conv2,
        skip.reshape(seqs, slab, half),
        cotangent.reshape(seqs, slab, half),
        gain_coarse.reshape(1, -1),
        gain_fine.reshape(1, -1),
    )
    wide = (seqs, 2 * slab, quarter)
    return decoded.reshape(wide), skip_grad.reshape(wide), trunk_grad


def solution(mesh):
    body = per_device_fused if fits(mesh) else per_device
    in_specs = (
        P(None, "seq", "tensor"),
        P("tensor", "seq"),
        P(),
        P(None, "seq", "tensor"),
        P("seq", None, "tensor"),
        P(None, "seq", "tensor"),
        P(),
        P(None, "seq", "tensor"),
        P(None, "seq", "tensor"),
    )
    out_specs = (P(None, "seq", "tensor"), P(None, "seq", "tensor"), P(None, "seq", "tensor"))
    return jax.shard_map(
        body, mesh=mesh, in_specs=in_specs, out_specs=out_specs, check_vma=False
    )
```

```python
import functools

import jax
import jax.numpy as jnp
from jax import lax
from jax.experimental import pallas as pl
from jax.experimental.pallas import tpu as pltpu
from jax.sharding import PartitionSpec as P

C_COARSE = 1536
C_FINE = 768


EPS = 1e-06


def extended(shard, sides, width):
    for axis, dim in sides:
        size, length = (lax.axis_size(axis), shard.shape[dim])
        up = [(i, (i + 1) % size) for i in range(size - 1)]
        down = [(j, i) for i, j in up]
        last = lax.slice_in_dim(shard, length - width, length, axis=dim)
        leading = lax.slice_in_dim(shard, 0, width, axis=dim)
        before = lax.ppermute(last, axis, up)
        after = lax.ppermute(leading, axis, down)
        shard = jnp.concatenate([before, shard, after], axis=dim)
    return shard


def matmul(left, right):
    return lax.dot_general(
        left, right, (((left.ndim - 1,), (0,)), ((), ())), preferred_element_type=jnp.float32
    )


def matmul_back(left, right):
    return lax.dot_general(
        left,
        right,
        (((left.ndim - 1,), (right.ndim - 1,)), ((), ())),
        preferred_element_type=jnp.float32,
    )


def activate(field, gain):
    scaled = field * lax.rsqrt(jnp.mean(field * field, axis=-1, keepdims=True) + EPS)
    return jax.nn.gelu(scaled * gain)


def widen(field):
    return extended(field, (("seq", 1),), 2)


def spread(field):
    return lax.all_gather(field, "tensor", axis=2, tiled=True)


def conv_rows(total, wide, piece):
    length = wide.shape[1] - 4
    for k in range(5):
        total = total + matmul(wide[:, k : k + length], piece[k])
    return total


def conv_back(wide_grad, piece):
    length = wide_grad.shape[1] - 4
    total = jnp.zeros((wide_grad.shape[0], length, piece.shape[1]), jnp.float32)
    for k in range(5):
        total = total + matmul_back(wide_grad[:, 4 - k : 4 - k + length], piece[k])
    return total


def norm_back(partial_grad, field_full, gain, rank, part):
    field = field_full.astype(jnp.float32)
    start = rank * part
    whole = lax.psum(partial_grad.astype(jnp.bfloat16), "tensor").astype(jnp.float32)

    def apply(value):
        return activate(value, gain)

    _, pull = jax.vjp(apply, field)
    return lax.dynamic_slice_in_dim(pull(whole)[0], start, part, 2)


def per_device(trunk, w_out, gain_coarse, w_conv1, w_up, skip, gain_fine, w_conv2, cotangent):
    rank = lax.axis_index("tensor")
    part_coarse = C_COARSE // lax.axis_size("tensor")
    part_fine = C_FINE // lax.axis_size("tensor")
    seqs = trunk.shape[0]
    slab = trunk.shape[1]
    out_w, up_w, conv2_w = (
        lax.all_gather(w_out, "seq", axis=1, tiled=True),
        lax.all_gather(w_up, "seq", axis=0, tiled=True),
        lax.all_gather(w_conv2, "seq", axis=1, tiled=True),
    )
    partial_proj = matmul(trunk, out_w)
    projected = lax.psum_scatter(
        partial_proj.astype(jnp.bfloat16), "tensor", scatter_dimension=2, tiled=True
    )
    projected_full = lax.all_gather(projected, "tensor", axis=2, tiled=True)
    act_coarse = activate(projected_full.astype(jnp.float32), gain_coarse).astype(jnp.bfloat16)
    coarse_wide = widen(act_coarse)
    empty_coarse = jnp.zeros((seqs, slab, part_coarse), jnp.float32)
    mixed_coarse = conv_rows(
        empty_coarse, coarse_wide, lax.all_gather(w_conv1, "seq", axis=1, tiled=True)
    )
    lifted = (projected.astype(jnp.float32) + mixed_coarse).astype(jnp.bfloat16)
    lifted_full = spread(lifted)
    upper = matmul(lifted_full, up_w).reshape(seqs, 2 * slab, part_fine)
    merged = (upper + skip.astype(jnp.float32)).astype(jnp.bfloat16)
    merged_full = spread(merged)
    act_fine = activate(merged_full.astype(jnp.float32), gain_fine).astype(jnp.bfloat16)
    fine_wide = widen(act_fine)
    empty_fine = jnp.zeros((seqs, 2 * slab, part_fine), jnp.float32)
    mixed_fine = conv_rows(empty_fine, fine_wide, conv2_w)
    decoded = (merged.astype(jnp.float32) + mixed_fine).astype(jnp.bfloat16)
    cot_wide = widen(cotangent)
    back_fine = conv_back(cot_wide, conv2_w)
    skip_grad = (
        cotangent.astype(jnp.float32)
        + norm_back(back_fine, merged_full, gain_fine, rank, part_fine)
    ).astype(jnp.bfloat16)
    folded = skip_grad.reshape(seqs, slab, 2 * part_fine)
    up_partial = matmul_back(folded, up_w.reshape(up_w.shape[0], 2 * part_fine))
    lifted_grad = lax.psum_scatter(
        up_partial.astype(jnp.bfloat16), "tensor", scatter_dimension=2, tiled=True
    )
    grad_wide = widen(lifted_grad)
    back_coarse = conv_back(grad_wide, lax.all_gather(w_conv1, "seq", axis=1, tiled=True))
    projected_grad = (
        lifted_grad.astype(jnp.float32)
        + norm_back(back_coarse, projected_full, gain_coarse, rank, part_coarse)
    ).astype(jnp.bfloat16)
    grad_full = spread(projected_grad)
    trunk_grad = matmul_back(grad_full, out_w).astype(jnp.bfloat16)
    return (decoded, skip_grad, trunk_grad)


PIECES = 8
Y_FIRST = 3
LINE = 4
HALO = 8


def fits(mesh):
    return mesh.shape["seq"] == 4 * LINE and mesh.shape["tensor"] == 2


def gelu_parts(u):
    c = 0.7978845608028654
    th = jnp.tanh(c * (u + 0.044715 * (u * u * u)))
    return 0.5 * (1.0 + th), th, c


def gelu(u):
    half, _, _ = gelu_parts(u)
    return u * half


def gelu_slope(u):
    half, th, c = gelu_parts(u)
    return half + 0.5 * u * (1.0 - th * th) * c * (1.0 + 3.0 * 0.044715 * (u * u))


def dot(a, b):
    return jnp.dot(a, b, preferred_element_type=jnp.float32)


def dot_t(a, b):
    return lax.dot_general(a, b, (((1,), (1,)), ((), ())), preferred_element_type=jnp.float32)


def fused_kernel(
    trunk, w_own, w2_own, skip, cot, gain_c, gain_f,
    decoded, skip_grad, trunk_grad,
    wb, w2, center, halo, ext, skipf, cotf, pp, pp_in, proj, act, accf, lifted, merged, actf,
    bf, bf_in, accd, sgf, sgb, ug, ug_in, lgf, lgc, lgk, bc, bc_in, pg,
    rsem, ssem, lsem, hs, hr, xs, xr,
):
    s = lax.axis_index("seq")
    x = lax.axis_index("tensor")
    z = s // 4
    y = (s // 2) % 2
    c = s % 2
    rows = ext.shape[0]
    per = rows // 2
    slab = per - 2 * HALO
    half = wb.shape[2]
    quarter = half // 2
    seqs = 2
    gain_c, gain_f = gain_c[...].reshape(1, -1), gain_f[...].reshape(1, -1)
    MESH = pl.DeviceIdType.MESH
    bf16 = jnp.bfloat16
    n_seq = 4 * LINE

    def near(dev):
        return {"seq": dev}

    ydev = s + 2 - 4 * y
    cdev = s + 1 - 2 * c
    xdev = {"tensor": 1 - x}

    own_w = pltpu.make_async_copy(
        w_own, wb.at[:, pl.ds(pl.multiple_of(s * 96, 96), 96), :], lsem.at[0]
    )
    own_w2 = pltpu.make_async_copy(
        w2_own, w2.at[:, pl.ds(pl.multiple_of(s * 48, 48), 48), :], lsem.at[1]
    )
    mine = [pltpu.make_async_copy(r, center.at[i], lsem.at[2 + i]) for i, r in enumerate((trunk, skip, cot))]
    for copy in [own_w2, own_w] + mine:
        copy.start()

    barrier = pltpu.get_barrier_semaphore()
    for dev in (near(ydev), near(cdev), xdev):
        pl.semaphore_signal(barrier, inc=1, device_id=dev, device_id_type=MESH)
    for ok, dev in ((z > 0, s - 4), (z < LINE - 1, s + 4), (s > 0, s - 1), (s < n_seq - 1, s + 1)):

        @pl.when(ok)
        def _(dev=dev):
            pl.semaphore_signal(barrier, inc=1, device_id=near(dev), device_id_type=MESH)

    one = jnp.int32(1)
    zero = jnp.int32(0)
    count = (
        3
        + jnp.where(z > 0, one, zero)
        + jnp.where(z < LINE - 1, one, zero)
        + jnp.where(s > 0, one, zero)
        + jnp.where(s < n_seq - 1, one, zero)
    )
    pl.semaphore_wait(barrier, count)

    def halo_copy(i, side, dev):
        lo = slab - 16 if side == 0 else 0
        return pltpu.make_async_remote_copy(
            src_ref=center.at[i, :, pl.ds(lo, 16), :],
            dst_ref=halo.at[i, side],
            send_sem=hs.at[i, side],
            recv_sem=hr.at[i, side],
            device_id=near(dev),
            device_id_type=MESH,
        )

    def ref(p, owner, wide):
        if wide:
            return w2.at[:, pl.ds(pl.multiple_of(owner * 48, 48), 48), :]
        return wb.at[p - 1, pl.ds(pl.multiple_of(owner * 96, 96), 96), :]

    def send(p, owner, wide, way, dev):
        return pltpu.make_async_remote_copy(
            src_ref=ref(p, owner, wide),
            dst_ref=ref(p, owner, wide),
            send_sem=ssem.at[p, owner, way],
            recv_sem=rsem.at[p, owner],
            device_id=near(dev),
            device_id_type=MESH,
        )

    def routes():
        out = []
        for d in range(LINE):
            for sign in (1, -1) if d else (0,):
                out.append((d, sign, False))
                out.append((d, sign, True))
        return out

    def each(p, d, sign, across, act_on):
        zz = z - sign * d
        base = s - 4 * sign * d
        owner = base + 2 - 4 * y if across else base
        there = (zz >= 0) & (zz < LINE) & (p >= 0) & (p < PIECES)
        for wide in (True, False):

            @pl.when(there & ((p == 0) if wide else (p > 0)))
            def _(wide=wide):
                act_on(p, owner, wide, d, sign, across)

    def targets(p, owner, wide, d, sign, across, do):
        first = False if wide else p == Y_FIRST

        def along():
            if sign >= 0:

                @pl.when(z < LINE - 1)
                def _():
                    do(send(p, owner, wide, 0, s + 4))

            if sign <= 0:

                @pl.when(z > 0)
                def _():
                    do(send(p, owner, wide, 1, s - 4))

        if across:
            if not wide:
                pl.when(first)(along)
        else:
            along()
            if d == 0 or wide:
                do(send(p, owner, wide, 2, ydev))
            else:

                @pl.when(jnp.logical_not(first))
                def _():
                    do(send(p, owner, wide, 2, ydev))

        do(send(p, owner, wide, 3, cdev))

    def forward(p, owner, wide, d, sign, across):
        if d or across:
            send(p, owner, wide, 3, cdev).wait_recv()
        targets(p, owner, wide, d, sign, across, lambda copy: copy.start())

    def drain(p, owner, wide, d, sign, across):
        targets(p, owner, wide, d, sign, across, lambda copy: copy.wait_send())

    def step(t):
        for d, sign, across in routes():
            each(t - d - (1 if across else 0), d, sign, across, forward)

    def from_core(p, wide):
        def body(i, carry):
            owner = 2 * i + 1 - c
            send(p, owner, wide, 3, cdev).wait_recv()
            return carry

        lax.fori_loop(0, 2 * LINE, body, 0)

    def exchange(i, src, dst):
        return pltpu.make_async_remote_copy(
            src_ref=src,
            dst_ref=dst,
            send_sem=xs.at[i],
            recv_sem=xr.at[i],
            device_id=xdev,
            device_id_type=MESH,
        )

    def loop(n, body):
        def run(i, carry):
            body(i)
            return carry

        lax.fori_loop(0, n, run, 0)

    own_w2.wait()
    own_w.wait()
    for copy in mine:
        copy.wait()
    for i in range(3):
        for side, ok, dev in ((0, s < n_seq - 1, s + 1), (1, s > 0, s - 1)):

            @pl.when(ok)
            def _(i=i, side=side, dev=dev):
                halo_copy(i, side, dev).start()

    loop(4, step)

    for i in range(3):
        for side, ok in ((0, s > 0), (1, s < n_seq - 1)):

            @pl.when(ok)
            def _(i=i, side=side):
                halo_copy(i, side, cdev).wait_recv()

            @pl.when(jnp.logical_not(ok))
            def _(i=i, side=side):
                halo[i, side] = jnp.zeros(halo.shape[2:], bf16)

    for i in range(3):
        for q in range(seqs):
            before = halo[i, 0, q].astype(jnp.float32)[16 - HALO :]
            after = halo[i, 1, q].astype(jnp.float32)[:HALO]
            whole = jnp.concatenate([before, center[i, q].astype(jnp.float32), after], axis=0)
            if i == 0:
                ext[pl.ds(q * per, per), :] = whole.astype(bf16)
            elif i == 1:
                skipf[pl.ds(q * per, per), :] = whole
            else:
                cotf[pl.ds(q * per, per), :] = whole

    def inside(start, size):
        r = start + lax.broadcasted_iota(jnp.int32, (size, 1), 0)
        at = jnp.where(r >= per, r - per, r) + s * slab - HALO
        return (at >= 0) & (at < n_seq * slab)

    lax.fori_loop(4, 6, lambda t, k: (step(t), k)[1], 0)
    from_core(0, True)
    from_core(1, False)

    def project(n):
        cols = pl.ds(pl.multiple_of(n * 256, 256), 256)
        pp[:, cols] = dot_t(ext[...], wb[0, cols, :]).astype(bf16)

    loop(2 * half // 256, project)
    send_pp = exchange(0, pp, pp_in)
    send_pp.start()

    step(jnp.int32(6))

    def roll(v, shift):
        return pltpu.roll(v, shift % rows, 0)

    c0 = cotf[:, :quarter]
    c1 = cotf[:, quarter:]
    b0, b1 = c0.astype(bf16), c1.astype(bf16)
    up0, up1 = roll(c0, -1).astype(bf16), roll(c1, -1).astype(bf16)
    dn0, dn1 = roll(c0, 1).astype(bf16), roll(c1, 1).astype(bf16)
    even = (up0, b1, b0, dn1, dn0)
    odd = (up1, up0, b1, b0, dn1)

    def back_fine(n):
        cols = pl.ds(pl.multiple_of(n * 256, 256), 256)
        for par, taps in ((0, even), (1, odd)):
            total = dot_t(taps[0], w2[0, cols, :])
            for k in range(1, 5):
                total = total + dot_t(taps[k], w2[k, cols, :])
            bf[par, :, cols] = total.astype(bf16)

    loop(half // 256, back_fine)
    send_bf = exchange(1, bf, bf_in)
    send_bf.start()

    send_pp.wait_recv()

    def norm(f):
        return lax.rsqrt(jnp.mean(f * f, axis=-1, keepdims=True) + EPS)

    def coarse(i):
        at = pl.ds(pl.multiple_of(i * 32, 32), 32)
        f = (pp[at, :].astype(jnp.float32) + pp_in[at, :].astype(jnp.float32)).astype(bf16).astype(jnp.float32)
        proj[at, :] = f
        a = gelu(f * norm(f) * gain_c)
        act[at, :] = jnp.where(inside(i * 32, 32), a, 0.0).astype(bf16)

    loop(rows // 32, coarse)
    xhalf = pl.ds(pl.multiple_of(x * half, half), half)
    accf[...] = proj[:, xhalf]

    def tap_ahead(k):
        from_core(2 + k, False)
        for n in range(half // 256):
            cols = pl.ds(n * 256, 256)
            accf[:, cols] += pltpu.roll(dot(act[...], wb[1 + k, :, cols]), lax.rem(rows + 2 - k, rows), 0)

    def tap_and_step(k):
        step(7 + k)
        tap_ahead(k)

    loop(4, tap_and_step)
    tap_ahead(jnp.int32(4))
    lifted[:, xhalf] = accf[...].astype(bf16)
    send_lifted = exchange(2, lifted.at[:, xhalf], lifted.at[:, xhalf])
    send_lifted.start()
    step(jnp.int32(11))
    from_core(7, False)
    exchange(2, lifted.at[:, pl.ds(pl.multiple_of((1 - x) * half, half), half)], lifted.at[:, pl.ds(pl.multiple_of((1 - x) * half, half), half)]).wait_recv()
    xq = pl.ds(pl.multiple_of(x * quarter, quarter), quarter)
    oq = pl.ds(pl.multiple_of((1 - x) * quarter, quarter), quarter)
    for n in range(half // 384):
        cols = pl.ds(n * 384, 384)
        m = (dot(lifted[...], wb[6, :, cols]) + skipf[:, cols]).astype(bf16)
        merged[n, :, xq] = m
        accd[:, cols] = m.astype(jnp.float32)
    send_merged = exchange(3, merged.at[:, :, xq], merged.at[:, :, xq])
    send_merged.start()
    send_bf.wait_recv()
    exchange(3, merged.at[:, :, oq], merged.at[:, :, oq]).wait_recv()

    def pull(f, gain, grad):
        r = norm(f)
        dn = grad * gelu_slope(f * r * gain) * gain
        return r * dn - f * (r * r * r * jnp.mean(dn * f, axis=-1, keepdims=True))

    def fine(i):
        at = pl.ds(pl.multiple_of(i * 32, 32), 32)
        for par in range(2):
            f = merged[par, at, :].astype(jnp.float32)
            u = f * norm(f) * gain_f
            actf[par, at, :] = jnp.where(inside(i * 32, 32), gelu(u), 0.0).astype(bf16)
            g = bf[par, at, :].astype(jnp.float32) + bf_in[par, at, :].astype(jnp.float32)
            df = pull(f, gain_f, g)
            mine = jnp.where(x == 0, df[:, :quarter], df[:, quarter:])
            cols = pl.ds(par * quarter, quarter)
            v = cotf[at, cols] + mine
            sgf[at, cols] = v
            sgb[at, cols] = v.astype(bf16)

    loop(rows // 32, fine)

    def up_back(which, out):
        def body(n):
            cols = pl.ds(pl.multiple_of(n * 256, 256), 256)
            wrow = pl.ds(pl.multiple_of(which * half + n * 256, 256), 256)
            out[:, cols] = dot_t(sgb[...], wb[6, wrow, :]).astype(bf16)

        loop(half // 256, body)

    up_back(1 - x, ug)
    send_ug = exchange(4, ug, ug_in)
    send_ug.start()
    send_lifted.wait_send()
    up_back(x, lifted.at[:, pl.ds(0, half)])
    for q in range(seqs):
        skip_grad[q] = sgf[pl.ds(q * per + HALO, slab), :].astype(bf16)
    send_ug.wait_recv()

    def meet(i):
        at = pl.ds(pl.multiple_of(i * 32, 32), 32)
        v = lifted[at, :half].astype(jnp.float32) + ug_in[at, :].astype(jnp.float32)
        lgf[at, :] = jnp.where(inside(i * 32, 32), v, 0.0).astype(bf16).astype(jnp.float32)

    loop(rows // 32, meet)
    for q in range(seqs):
        lgc[pl.ds(q * slab, slab), xhalf] = lgf[pl.ds(q * per + HALO, slab), :].astype(bf16)
    send_lg = exchange(5, lgc.at[:, xhalf], lgc.at[:, xhalf])
    send_lg.start()

    def shifted(k):
        v = pltpu.roll(lgf[...], lax.rem(rows + k - 2, rows), 0)
        for q in range(seqs):
            lgk[k, pl.ds(q * slab, slab), :] = v[q * per + HALO : q * per + HALO + slab].astype(bf16)

    loop(5, shifted)

    def back_coarse(n):
        cols = pl.ds(pl.multiple_of(n * 256, 256), 256)
        total = dot_t(lgk[0], wb[1, cols, :])
        for k in range(1, 5):
            total = total + dot_t(lgk[k], wb[1 + k, cols, :])
        bc[:, cols] = total.astype(bf16)

    loop(2 * half // 256, back_coarse)
    send_bc = exchange(6, bc, bc_in)
    send_bc.start()

    e = {}
    for k in range(5):
        e[k] = [dot(actf[par], w2[k]) for par in range(2)]
        for par in range(2):
            fine_at = par - (k - 2)
            q = fine_at % 2
            shift = (fine_at - q) // 2
            v = e[k][par] if shift == 0 else roll(e[k][par], shift)
            accd[:, q * quarter : (q + 1) * quarter] += v
    for q in range(seqs):
        decoded[q] = accd[pl.ds(q * per + HALO, slab), :].astype(bf16)

    oth = pl.ds(pl.multiple_of((1 - x) * half, half), half)
    exchange(5, lgc.at[:, oth], lgc.at[:, oth]).wait_recv()
    send_bc.wait_recv()
    for q in range(seqs):

        def last(i, q=q):
            at = pl.ds(pl.multiple_of(q * slab + i * 32, 32), 32)
            f = proj[pl.ds(pl.multiple_of(q * per + HALO + i * 32, 8), 32), :]
            g = bc[at, :].astype(jnp.float32) + bc_in[at, :].astype(jnp.float32)
            pg[at, :] = (lgc[at, :].astype(jnp.float32) + pull(f, gain_c, g)).astype(bf16)

        loop(slab // 32, last)
    for n in range(half // 256):
        cols = pl.ds(n * 256, 256)
        v = dot(pg[...], wb[0, :, cols]).astype(bf16)
        for q in range(seqs):
            trunk_grad[q, :, cols] = v[q * slab : (q + 1) * slab]

    for copy in (send_pp, send_bf, send_merged, send_ug, send_lg, send_bc):
        copy.wait_send()
    for i in range(3):
        for side, ok, dev in ((0, s < n_seq - 1, s + 1), (1, s > 0, s - 1)):

            @pl.when(ok)
            def _(i=i, side=side, dev=dev):
                halo_copy(i, side, dev).wait_send()

    def finish(p):
        for d, sign, across in routes():
            each(p, d, sign, across, drain)

    loop(PIECES, finish)


def per_device_fused(trunk, w_out, gain_coarse, w_conv1, w_up, skip, gain_fine, w_conv2, cotangent):
    seqs, slab, half = trunk.shape
    quarter = half // 2
    n = lax.axis_size("seq")
    rows = seqs * (slab + 2 * HALO)
    w_own = jnp.concatenate([w_out.T[None], w_conv1, w_up.reshape(1, -1, half)], axis=0)
    bf16, f32 = jnp.bfloat16, jnp.float32
    V = pltpu.VMEM
    out = jax.ShapeDtypeStruct((seqs, slab, half), bf16)
    vm = pl.BlockSpec(memory_space=pltpu.VMEM)
    anyw = pl.BlockSpec(memory_space=pl.ANY)
    decoded, skip_grad, trunk_grad = pl.pallas_call(
        fused_kernel,
        out_shape=(out, out, out),
        in_specs=[anyw] * 5 + [vm] * 2,
        out_specs=(vm, vm, vm),
        scratch_shapes=[
            V((7, 2 * half, half), bf16),
            V((5, half, quarter), bf16),
            V((3, seqs, slab, half), bf16),
            V((3, 2, seqs, 16, half), bf16),
            V((rows, half), bf16),
            V((rows, half), f32),
            V((rows, half), f32),
            V((rows, 2 * half), bf16),
            V((rows, 2 * half), bf16),
            V((rows, 2 * half), f32),
            V((rows, 2 * half), bf16),
            V((rows, half), f32),
            V((rows, 2 * half), bf16),
            V((2, rows, half), bf16),
            V((2, rows, half), bf16),
            V((2, rows, half), bf16),
            V((2, rows, half), bf16),
            V((rows, half), f32),
            V((rows, half), f32),
            V((rows, half), bf16),
            V((rows, half), bf16),
            V((rows, half), bf16),
            V((rows, half), f32),
            V((seqs * slab, 2 * half), bf16),
            V((5, seqs * slab, half), bf16),
            V((seqs * slab, 2 * half), bf16),
            V((seqs * slab, 2 * half), bf16),
            V((seqs * slab, 2 * half), bf16),
            pltpu.SemaphoreType.DMA((PIECES, n)),
            pltpu.SemaphoreType.DMA((PIECES, n, 4)),
            pltpu.SemaphoreType.DMA((5,)),
            pltpu.SemaphoreType.DMA((3, 2)),
            pltpu.SemaphoreType.DMA((3, 2)),
            pltpu.SemaphoreType.DMA((7,)),
            pltpu.SemaphoreType.DMA((7,)),
        ],
        compiler_params=pltpu.CompilerParams(
            collective_id=0, has_side_effects=True, vmem_limit_bytes=56 * 1024 * 1024
        ),
    )(
        trunk,
        w_own,
        w_conv2,
        skip.reshape(seqs, slab, half),
        cotangent.reshape(seqs, slab, half),
        gain_coarse,
        gain_fine,
    )
    wide = (seqs, 2 * slab, quarter)
    return decoded.reshape(wide), skip_grad.reshape(wide), trunk_grad


def solution(mesh):
    body = per_device_fused if fits(mesh) else per_device
    in_specs = (
        P(None, "seq", "tensor"),
        P("tensor", "seq"),
        P(),
        P(None, "seq", "tensor"),
        P("seq", None, "tensor"),
        P(None, "seq", "tensor"),
        P(),
        P(None, "seq", "tensor"),
        P(None, "seq", "tensor"),
    )
    out_specs = (P(None, "seq", "tensor"), P(None, "seq", "tensor"), P(None, "seq", "tensor"))
    return jax.shard_map(
        body, mesh=mesh, in_specs=in_specs, out_specs=out_specs, check_vma=False
    )
```
